512 devices in a mesh: dp: 128 (over y_lo, z, x, core), tensor: 4 (over y_hi).
Axes of the slice: x: 4, y: 8 (y_hi: 4, y_lo: 2; y = y_hi * 2 + y_lo), z: 8, core: 2. Of those that a mesh axis runs over, the one named last changes fastest.
Arguments:
- pooled_caption_states: bfloat16 [8192, 1152], P('dp', 'tensor'), may hold values from -6 to 6
- first_dense_matrix: bfloat16 [1152, 3072], P(None, 'tensor'), may hold values from -0.1875 to 0.1875
- first_dense_offset: float32 [3072], P('tensor'), may hold values from -4 to 4
- second_dense_matrix: bfloat16 [3072, 1152], P('tensor'), may hold values from -0.109375 to 0.109375
- second_dense_offset: float32 [1152], replicated, may hold values from -4 to 4
- picture_vectors_unnormed: bfloat16 [8192, 1152], P('dp'), may hold values from -6 to 6
- matching_caption_position: int32 [8192], P('dp'), may hold values from 0 to 8191, each once
- learned_sharpness: float32 [1], replicated, may hold values from 5 to 20
- learned_score_offset: float32 [1], replicated, may hold values from -5 to -2
Outputs:
- text_grad: float32 [8192, 1152], P(('dp', 'tensor'))
- image_grad: float32 [8192, 1152], P(('dp', 'tensor'))
The draws below stay inside these ranges and needn't reach their ends.
Inputs may be any that keep to these rules, and one draw needn't show every extreme that they name: matching_caption_position is a permutation: every text row is the positive of exactly one image.
All inputs are finite; a program needn't handle non-finite values.
Results may differ from the reference program's by a relative error of at most 0.004.
Values may be sent and summed in bfloat16 or wider, within the bound.
No kernel may reach another device: no remote copies, remote signals or barrier semaphores. Data moves between devices by JAX's collectives and lax.ppermute only.
A program may use at most 64 MiB of HBM per device.

```python
import math
import jax
import jax.numpy as jnp
from jax import lax

D = 1152
FF = 3072
BATCH = 8192


def levels(key, shape, cuts, smallest, top_value):
    def one(dim, parts):
        steps = jax.random.uniform(jax.random.fold_in(jax.random.fold_in(key, 6), dim), (parts,), jnp.float32, smallest / len(cuts), top_value / len(cuts))
        return jnp.repeat(jnp.exp(steps), shape[dim] // parts).reshape((-1,) + (1,) * (len(shape) - dim - 1))

    level = one(*cuts[0])
    for cut in cuts[1:]:
        level = level * one(*cut)
    return level


def gaussian(own_key, shape, deviation, reach, split=(), kind=jnp.bfloat16):
    result = jax.random.normal(own_key, shape, jnp.float32) * deviation
    if len(split) > 0:
        result = levels(own_key, shape, split, -0.22, 0.18) * result
    return jnp.clip(result, min=-reach, max=reach).astype(kind)


def setup_inputs(seed: int = 0) -> dict:
    key_list = jax.random.split(jax.random.key(seed), 10)
    pooled_caption_states = gaussian(key_list[0], (BATCH, D), 1.0, 6.0, ((0, 128), (1, 4)))
    first_dense_matrix = gaussian(key_list[1], (D, FF), D ** -0.5, 0.1875, ((1, 4),))
    first_dense_offset = gaussian(key_list[2], (FF,), 1.0, 4.0, ((0, 4),), jnp.float32)
    second_dense_matrix = gaussian(key_list[3], (FF, D), FF ** -0.5, 0.109375, ((0, 4),))
    second_dense_offset = gaussian(key_list[4], (D,), 1.0, 4.0, (), jnp.float32)
    picture_vectors_unnormed = gaussian(key_list[5], (BATCH, D), 1.0, 6.0, ((0, 128),))
    matching_caption_position = jax.random.permutation(key_list[6], BATCH).astype(jnp.int32)
    learned_sharpness = jnp.clip(jnp.exp(jax.random.uniform(key_list[7], (1,), jnp.float32, math.log(5.0), math.log(20.0))), 5.0, 20.0)
    learned_score_offset = jnp.clip(jax.random.uniform(key_list[8], (1,), jnp.float32, -5.0, -2.0), -5.0, -2.0)
    return dict(pooled_caption_states=pooled_caption_states, first_dense_matrix=first_dense_matrix, first_dense_offset=first_dense_offset, second_dense_matrix=second_dense_matrix, second_dense_offset=second_dense_offset, picture_vectors_unnormed=picture_vectors_unnormed, matching_caption_position=matching_caption_position, learned_sharpness=learned_sharpness, learned_score_offset=learned_score_offset)


EPSILON = 1e-06

def layer_norm(values):
    widened = values.astype(jnp.float32)
    centred = widened - lax.optimization_barrier(jnp.mean(widened, axis=-1, keepdims=True))
    variance = lax.optimization_barrier(jnp.mean(centred * centred, axis=-1, keepdims=True))
    return (centred * lax.rsqrt(variance + EPSILON)).astype(jnp.bfloat16)

def unit_rows(values):
    squared = lax.optimization_barrier(jnp.sum(values * values, axis=-1, keepdims=True))
    return (values * lax.rsqrt(squared + EPSILON)).astype(jnp.bfloat16)

def couple_losses(layer_group, group_numbers, picture_direction, matching_caption_position, sharpness_factor, additive_constant):
    similarity_matrix = sharpness_factor * lax.dot_general(layer_group, picture_direction, (((1,), (1,)), ((), ())), preferred_element_type=jnp.float32) + additive_constant
    matched = matching_caption_position[None, :] == group_numbers[:, None]
    label_sign_matrix = jnp.where(matched, 1.0, -1.0).astype(jnp.float32)
    sigmoid_coefficients = (-sharpness_factor * label_sign_matrix * jax.nn.sigmoid(-label_sign_matrix * similarity_matrix)).astype(jnp.bfloat16)
    caption_share = jnp.dot(sigmoid_coefficients, picture_direction, preferred_element_type=jnp.float32)
    picture_share = lax.dot_general(sigmoid_coefficients, layer_group, (((0,), (0,)), ((), ())), preferred_element_type=jnp.float32)
    return (caption_share, picture_share)

def reference(pooled_caption_states, first_dense_matrix, first_dense_offset, second_dense_matrix, second_dense_offset, picture_vectors_unnormed, matching_caption_position, learned_sharpness, learned_score_offset):
    normed = layer_norm(pooled_caption_states)
    hidden = jax.nn.gelu(jnp.dot(normed, first_dense_matrix, preferred_element_type=jnp.float32) + first_dense_offset, approximate=True).astype(jnp.bfloat16)
    branch = jnp.dot(hidden, second_dense_matrix, preferred_element_type=jnp.float32)
    text_unit = unit_rows(pooled_caption_states.astype(jnp.float32) + branch + second_dense_offset)
    picture_direction = unit_rows(picture_vectors_unnormed.astype(jnp.float32))
    sharpness_factor = learned_sharpness[0]
    additive_constant = learned_score_offset[0]
    total_rows = pooled_caption_states.shape[0]
    width = pooled_caption_states.shape[1]
    block_rows = min(512, total_rows)
    block_count = total_rows // block_rows

    def one_block(image_total, index):
        first_row = index * block_rows
        layer_group = lax.dynamic_slice_in_dim(text_unit, first_row, block_rows, 0)
        group_numbers = first_row + jnp.arange(block_rows, dtype=jnp.int32)
        caption_share, picture_share = couple_losses(layer_group, group_numbers, picture_direction, matching_caption_position, sharpness_factor, additive_constant)
        return (image_total + picture_share, caption_share)
    image_total, text_parts = lax.scan(one_block, jnp.zeros((total_rows, width), jnp.float32), jnp.arange(block_count, dtype=jnp.int32))
    text_grad = text_parts.reshape(total_rows, width)
    return (text_grad, image_total)
```

```python
import jax
import jax.numpy as jnp
from jax import lax
from jax.sharding import Mesh, PartitionSpec as P

EPSILON = 1e-06
ROWS = ("yl", "z", "x", "core")
BF16 = jnp.bfloat16
F32 = jnp.float32


def spread(block, axes):
    count = lax.axis_size(axes)
    return lax.all_to_all(jnp.broadcast_to(block[None], (count,) + block.shape), axes, 0, 0)


def layer_norm(values):
    widened = values.astype(F32)
    centred = widened - jnp.mean(widened, axis=-1, keepdims=True)
    variance = jnp.mean(centred * centred, axis=-1, keepdims=True)
    return (centred * lax.rsqrt(variance + EPSILON)).astype(BF16)


def unit_rows(values):
    squared = jnp.sum(values * values, axis=-1, keepdims=True)
    return (values * lax.rsqrt(squared + EPSILON)).astype(BF16)


def shards(tokens, w1, b1, w2, b2, pictures, matching, sharpness, offset):
    scale, shift = sharpness[0], offset[0]
    t = lax.axis_index("t")
    x, core = lax.axis_index("x"), lax.axis_index("core")
    width = pictures.shape[1]

    image_unit = unit_rows(pictures.astype(F32))
    lane = lax.broadcasted_iota(jnp.int32, (matching.shape[0], 128), 1)
    digits = jnp.where(lane == 0, matching[:, None] // 128, jnp.where(lane == 1, matching[:, None] % 128, 0))
    packed = jnp.concatenate([image_unit, digits.astype(BF16)], axis=1)
    images = lax.all_gather(packed, ("x", "core"), axis=0, tiled=True)

    gathered = spread(tokens, "t")
    gathered = jnp.transpose(gathered, (1, 0, 2)).reshape(tokens.shape[0], width)
    normed = layer_norm(gathered)
    hidden = jax.nn.gelu(
        jnp.dot(normed, w1, preferred_element_type=F32) + b1, approximate=True
    ).astype(BF16)
    partial = jnp.dot(hidden, w2, preferred_element_type=F32)
    own = tokens.shape[0] // lax.axis_size("t")
    partial = lax.all_to_all(partial.reshape(-1, own, width), "t", 0, 0)
    residual = lax.dynamic_slice_in_dim(gathered, t * own, own, 0).astype(F32)
    text_own = unit_rows(residual + jnp.sum(partial, axis=0) + b2)
    text = spread(text_own, ("yl", "z"))
    groups = text.shape[0]
    text = text.reshape(groups * own, width)

    image = images[:, :width]
    position = images[:, width].astype(F32) * 128.0 + images[:, width + 1].astype(F32)
    block = lax.axis_size("core") * lax.axis_size("x") * tokens.shape[0]
    first = (x * lax.axis_size("core") + core) * tokens.shape[0] + t * own
    number = jnp.arange(groups * own, dtype=jnp.int32)
    ids = (number // own) * block + first + number % own
    matched = position.astype(jnp.int32)[:, None] == ids[None, :]
    scores = scale * lax.dot_general(
        image, text, (((1,), (1,)), ((), ())), preferred_element_type=F32
    ) + shift
    sign = jnp.where(matched, 1.0, -1.0).astype(F32)
    weights = (-scale * sign * jax.nn.sigmoid(-sign * scores)).astype(BF16)
    text_share = lax.dot_general(weights, image, (((0,), (0,)), ((), ())), preferred_element_type=F32)
    image_share = jnp.dot(weights, text, preferred_element_type=F32)

    text_parts = lax.all_to_all(
        text_share.astype(BF16).reshape(groups, own, width), ("yl", "z"), 0, 0
    )
    text_grad = jnp.sum(text_parts.astype(F32), axis=0)
    sized = image_share.reshape(lax.axis_size("x"), lax.axis_size("core"), lax.axis_size("t"), own, width)
    away = lax.dynamic_index_in_dim(sized, 1 - core, 1, keepdims=False).astype(BF16)
    mine = lax.dynamic_index_in_dim(sized, core, 1, keepdims=False)
    came = lax.ppermute(away, "core", [(0, 1), (1, 0)])
    pair = (mine + came.astype(F32)).astype(BF16).reshape(-1, own, width)
    image_parts = lax.all_to_all(pair, ("x", "t"), 0, 0)
    image_grad = jnp.sum(image_parts.astype(F32), axis=0)
    return text_grad, image_grad


def solution(mesh):
    fine = Mesh(mesh.devices.reshape(2, 8, 4, 2, 4), ROWS + ("t",))
    return jax.shard_map(
        shards,
        mesh=fine,
        in_specs=(
            P(ROWS, "t"),
            P(None, "t"),
            P("t"),
            P("t", None),
            P(),
            P(ROWS, None),
            P(ROWS),
            P(),
            P(),
        ),
        out_specs=(P(ROWS + ("t",), None), P(ROWS + ("t",), None)),
        check_vma=False,
    )
```

```python
import functools

import jax
import jax.numpy as jnp
from jax import lax
from jax.experimental import pallas as pl
from jax.experimental.pallas import tpu as pltpu
from jax.sharding import Mesh, PartitionSpec as P

EPSILON = 1e-06
ROWS = ("yl", "z", "x", "core")
ALL = ROWS + ("t",)
SIZES = dict(yl=2, z=8, x=4, core=2, t=4)
BF16 = jnp.bfloat16
F32 = jnp.float32
LANES = 128
VMEM = pl.BlockSpec(memory_space=pltpu.VMEM)
SMEM = pl.BlockSpec(memory_space=pltpu.SMEM)


def nt(a, b):
    return lax.dot_general(a, b, (((1,), (1,)), ((), ())), preferred_element_type=F32)


def nn(a, b):
    return jnp.dot(a, b, preferred_element_type=F32)


def call(kernel, outs, operands, scalars=0, flops=0):
    return pl.pallas_call(
        kernel,
        out_shape=outs,
        in_specs=[SMEM] * scalars + [VMEM] * (len(operands) - scalars),
        out_specs=jax.tree.map(lambda _: VMEM, outs),
        compiler_params=pltpu.CompilerParams(vmem_limit_bytes=40 * 2**20),
        cost_estimate=pl.CostEstimate(flops=flops, bytes_accessed=100_000, transcendentals=0),
    )(*operands)


def spread(block, axes):
    count = lax.axis_size(axes)
    return lax.all_to_all(jnp.broadcast_to(block[None], (count,) + block.shape), axes, 0, 0)


def swap_cores(block):
    return lax.ppermute(block, "core", [(0, 1), (1, 0)])


def from_behind(block, by):
    length = lax.axis_size("x")
    return lax.ppermute(block, "x", [(i, (i + by) % length) for i in range(length)])


def grad_groups():
    yl, z, x, core, t = (SIZES[a] for a in ALL)

    def flat(i, j, k, c, m):
        return (((i * z + j) * x + k) * core + c) * t + m

    text = [[flat(i, j, k, 0, m) for i in range(yl) for j in range(z)] for k in range(x) for m in range(t)]
    image = [[flat(i, j, k, 1, m) for k in range(x) for m in range(t)] for i in range(yl) for j in range(z)]
    return text + image


def unit(values):
    squared = jnp.sum(values * values, axis=-1, keepdims=True)
    return (values * lax.rsqrt(squared + EPSILON)).astype(BF16)


def pack_kernel(pictures, position, packed):
    width = pictures.shape[1]
    packed[:, :width] = unit(pictures[...].astype(F32))
    where = position[...]
    lane = lax.broadcasted_iota(jnp.int32, (where.shape[0], LANES), 1)
    digits = jnp.where(lane == 0, where // LANES, jnp.where(lane == 1, where % LANES, 0))
    packed[:, width:] = digits.astype(F32).astype(BF16)


def ffn_kernel(first, gathered, w1, b1, w2, b2, partial):
    parts = [gathered[k].astype(F32) for k in range(gathered.shape[0])]
    tokens = jnp.concatenate(parts, axis=1)
    centred = tokens - jnp.mean(tokens, axis=-1, keepdims=True)
    variance = jnp.mean(centred * centred, axis=-1, keepdims=True)
    normed = (centred * lax.rsqrt(variance + EPSILON)).astype(BF16)
    hidden = jax.nn.gelu(nn(normed, w1[...]) + b1[...], approximate=True).astype(BF16)
    branch = nn(hidden, w2[...])
    kept = jnp.where(first[0] == 0, tokens + b2[...], 0.0)
    partial[...] = (branch + kept).reshape(partial.shape)


def text_kernel(parts, copies):
    total = parts[0]
    for k in range(1, parts.shape[0]):
        total = total + parts[k]
    row = unit(total)
    for k in range(copies.shape[0]):
        copies[k] = row


def pair_kernel(place, numbers, text_own, text_other, image_own, image_other, out):
    groups, _, own, width = out.shape
    x, core, t = place[0], place[1], place[2]
    scale, shift = numbers[0], numbers[1]
    ring, tensor = SIZES["x"], SIZES["t"]
    block = tensor * own
    lane = lax.broadcasted_iota(jnp.int32, (8, LANES), 1)
    digit = jnp.where(lane == 0, float(LANES), jnp.where(lane == 1, 1.0, 0.0)).astype(BF16)

    def ids(shape, dim, which):
        row = lax.broadcasted_iota(jnp.int32, shape, dim)
        first = (x * 2 + which) * block + t * own
        return ((row // own) * (ring * 2 * block) + first + row % own).astype(F32)

    def weights(a, b, match):
        scores = scale * nt(a, b) + shift
        score = jnp.where(match, -scores, scores)
        size = jnp.where(match, -scale, scale)
        return (size / (1.0 + jnp.exp(-score))).astype(BF16)

    texts = ((text_own, core), (text_other, 1 - core))
    images = ((image_own, core), (image_other, 1 - core))
    many = groups * own

    @pl.when(core == 0)
    def _():
        for which, (text, from_core) in enumerate(texts):
            a = text[...].reshape(many, width)
            total = None
            for image, _ in images:
                b = image[:, :width]
                position = nt(digit, image[:, width:])[:1]
                match = ids((many, 1), 0, from_core) == position
                part = nn(weights(a, b, match), b)
                total = part if total is None else total + part
            out[:, which] = total.astype(BF16).reshape(groups, own, width)

    @pl.when(core == 1)
    def _():
        for which, (image, from_core) in enumerate(images):
            a = image[:, :width]
            position = nt(image[:, width:], digit)[:, :1]
            total = None
            for text, text_core in texts:
                b = text[...].reshape(many, width)
                match = position == ids((1, many), 1, text_core)
                part = nn(weights(a, b, match), b)
                total = part if total is None else total + part
            total = total.astype(BF16)
            for k in range(ring):
                at = lax.rem(x + ring - k, ring)
                rows = total[k * block : (k + 1) * block].reshape(tensor, own, width)
                out[pl.ds(at * tensor, tensor), 1 - which] = rows


def sum_kernel(core, parts, keep, send):
    def total(which):
        value = parts[0, which].astype(F32)
        for k in range(1, parts.shape[0]):
            value = value + parts[k, which].astype(F32)
        return value

    first, second = total(0), total(1)
    keep[...] = jnp.where(core[0] == 0, first, second)
    send[...] = jnp.where(core[0] == 0, second, first)


def shards(tokens, w1, b1, w2, b2, pictures, matching, sharpness, offset):
    x, core, t = (lax.axis_index(a).astype(jnp.int32) for a in ("x", "core", "t"))
    place = jnp.stack([x, core, t])
    rows, width = pictures.shape
    tensor, ring = lax.axis_size("t"), lax.axis_size("x")
    own = rows // tensor
    groups = lax.axis_size(("yl", "z"))

    gathered = spread(tokens, "t")
    packed = call(
        pack_kernel,
        jax.ShapeDtypeStruct((rows, width + LANES), BF16),
        (pictures, matching[:, None]),
    )
    moved = [from_behind(packed, k) for k in range(1, ring)]
    partial = call(
        ffn_kernel,
        jax.ShapeDtypeStruct((tensor, own, width), F32),
        (t[None], gathered, w1, b1[None], w2, b2[None]),
        scalars=1,
    )
    partial, packed, *moved = lax.optimization_barrier((partial, packed, *moved))
    parts = lax.all_to_all(partial, "t", 0, 0)
    image_own = jnp.concatenate([packed] + moved, axis=0)
    image_other = swap_cores(image_own)
    parts, image_other = lax.optimization_barrier((parts, image_other))
    copies = call(text_kernel, jax.ShapeDtypeStruct((groups, own, width), BF16), (parts,))
    text_own = lax.all_to_all(copies, ("yl", "z"), 0, 0)
    text_other = swap_cores(text_own)
    numbers = jnp.concatenate([sharpness, offset])
    shares = call(
        pair_kernel,
        jax.ShapeDtypeStruct((groups, 2, own, width), BF16),
        (place, numbers, text_own, text_other, image_own, image_other),
        scalars=2,
        flops=1_200_000_000,
    )
    shares = lax.all_to_all(shares, ALL, 0, 0, axis_index_groups=grad_groups())
    half = jax.ShapeDtypeStruct((own, width), F32)
    keep, send = call(sum_kernel, (half, half), (core[None], shares), scalars=1)
    came = swap_cores(send)
    return jnp.where(core == 0, keep, came), jnp.where(core == 0, came, keep)


def solution(mesh):
    fine = Mesh(mesh.devices.reshape([SIZES[a] for a in ALL]), ALL)
    return jax.shard_map(
        shards,
        mesh=fine,
        in_specs=(
            P(ROWS, "t"),
            P(None, "t"),
            P("t"),
            P("t", None),
            P(),
            P(ROWS, None),
            P(ROWS),
            P(),
            P(),
        ),
        out_specs=(P(ALL, None), P(ALL, None)),
        check_vma=False,
    )
```

```python
import functools

import jax
import jax.numpy as jnp
from jax import lax
from jax.experimental import pallas as pl
from jax.experimental.pallas import tpu as pltpu
from jax.sharding import Mesh, PartitionSpec as P

EPSILON = 1e-06
ROWS = ("yl", "z", "x", "core")
ALL = ROWS + ("t",)
SIZES = dict(yl=2, z=8, x=4, core=2, t=4)
BF16 = jnp.bfloat16
F32 = jnp.float32
LANES = 128
VMEM = pl.BlockSpec(memory_space=pltpu.VMEM)
HBM = pl.BlockSpec(memory_space=pl.ANY)
FULL = 55_000_000
SMEM = pl.BlockSpec(memory_space=pltpu.SMEM)


def nt(a, b):
    return lax.dot_general(a, b, (((1,), (1,)), ((), ())), preferred_element_type=F32)


def nn(a, b):
    return jnp.dot(a, b, preferred_element_type=F32)


def call(kernel, outs, operands, scalars=0, flops=0, specs=None, out_specs=None, scratch=(), room=2**25):
    return pl.pallas_call(
        kernel,
        out_shape=outs,
        in_specs=specs or [SMEM] * scalars + [VMEM] * (len(operands) - scalars),
        out_specs=out_specs or jax.tree.map(lambda _: VMEM, outs),
        scratch_shapes=scratch,
        compiler_params=pltpu.CompilerParams(vmem_limit_bytes=room),
        cost_estimate=pl.CostEstimate(flops=flops, bytes_accessed=100_000, transcendentals=0),
    )(*operands)


def swap_cores(block):
    return lax.ppermute(block, "core", [(0, 1), (1, 0)])


def from_behind(block, by):
    length = lax.axis_size("x")
    return lax.ppermute(block, "x", [(i, (i + by) % length) for i in range(length)])


def grad_groups():
    yl, z, x, core, t = (SIZES[a] for a in ALL)

    def flat(i, j, k, c, m):
        return (((i * z + j) * x + k) * core + c) * t + m

    text = [[flat(i, j, k, 0, m) for i in range(yl) for j in range(z)] for k in range(x) for m in range(t)]
    image = [[flat(i, j, k, 1, m) for k in range(x) for m in range(t)] for i in range(yl) for j in range(z)]
    return text + image


def unit(values):
    squared = jnp.sum(values * values, axis=-1, keepdims=True)
    return (values * lax.rsqrt(squared + EPSILON)).astype(BF16)


def pack_kernel(pictures, small, packed):
    count, width = pictures.shape
    packed[:, :width] = unit(pictures[...].astype(F32))
    down = lax.broadcasted_iota(jnp.int32, (count, LANES), 0)
    lane = lax.broadcasted_iota(jnp.int32, (count, LANES), 1)
    where = jnp.sum(jnp.where(down == lane, small[:, :LANES], 0.0), axis=1, keepdims=True).astype(jnp.int32)
    digits = jnp.where(lane == 0, where // LANES, jnp.where(lane == 1, where % LANES, 0))
    packed[:, width:] = digits.astype(F32).astype(BF16)


def ffn_kernel(gathered, small, w1, w2, partial, w1_near, w2_near, sems):
    first = pltpu.make_async_copy(w1, w1_near, sems.at[0])
    second = pltpu.make_async_copy(w2, w2_near, sems.at[1])
    first.start()
    second.start()
    hid = w1.shape[1]
    b1, b2 = small[:, LANES : LANES + hid], small[:, LANES + hid :]
    count = gathered.shape[0]
    tokens = jnp.concatenate([gathered[k].astype(F32) for k in range(count)], axis=1)
    centred = tokens - jnp.mean(tokens, axis=-1, keepdims=True)
    variance = jnp.mean(centred * centred, axis=-1, keepdims=True)
    normed = (centred * lax.rsqrt(variance + EPSILON)).astype(BF16)
    first.wait()
    hidden = jax.nn.gelu(nn(normed, w1_near[...]) + b1, approximate=True).astype(BF16)
    second.wait()
    branch = nn(hidden, w2_near[...])
    total = branch + (tokens + b2) * (1.0 / count)
    partial[...] = total.reshape(partial.shape).astype(partial.dtype)


def text_kernel(parts, copies):
    total = parts[0].astype(F32)
    for k in range(1, parts.shape[0]):
        total = total + parts[k].astype(F32)
    row = unit(total)
    for k in range(copies.shape[0]):
        copies[k] = row


def pair_kernel(place, numbers, text_own, text_other, image_own, image_other, out):
    groups, _, own, width = out.shape
    x, core, t = place[0], place[1], place[2]
    scale, shift = numbers[0], numbers[1]
    ring, tensor = SIZES["x"], SIZES["t"]
    block = tensor * own
    lane = lax.broadcasted_iota(jnp.int32, (8, LANES), 1)
    digit = jnp.where(lane == 0, float(LANES), jnp.where(lane == 1, 1.0, 0.0)).astype(BF16)

    def ids(shape, dim, which):
        row = lax.broadcasted_iota(jnp.int32, shape, dim)
        first = (x * 2 + which) * block + t * own
        return ((row // own) * (ring * 2 * block) + first + row % own).astype(F32)

    def weights(a, b, match):
        scores = scale * nt(a, b) + shift
        score = jnp.where(match, -scores, scores)
        size = jnp.where(match, -scale, scale)
        return (size / (1.0 + jnp.exp(-score))).astype(BF16)

    texts = ((text_own, core), (text_other, 1 - core))
    images = ((image_own, core), (image_other, 1 - core))
    many = groups * own

    @pl.when(core == 0)
    def _():
        for which, (text, from_core) in enumerate(texts):
            a = text[...].reshape(many, width)
            total = None
            for image, _ in images:
                b = image[:, :width]
                position = nt(digit, image[:, width:])[:1]
                match = ids((many, 1), 0, from_core) == position
                part = nn(weights(a, b, match), b)
                total = part if total is None else total + part
            out[:, which] = total.astype(BF16).reshape(groups, own, width)

    @pl.when(core == 1)
    def _():
        for which, (image, from_core) in enumerate(images):
            a = image[:, :width]
            position = nt(image[:, width:], digit)[:, :1]
            total = None
            for text, text_core in texts:
                b = text[...].reshape(many, width)
                match = position == ids((1, many), 1, text_core)
                part = nn(weights(a, b, match), b)
                total = part if total is None else total + part
            total = total.astype(BF16)
            for k in range(ring):
                at = lax.rem(x + ring - k, ring)
                rows = total[k * block : (k + 1) * block].reshape(tensor, own, width)
                out[pl.ds(at * tensor, tensor), 1 - which] = rows


def sum_kernel(parts, total):
    value = parts[0].astype(F32)
    for k in range(1, parts.shape[0]):
        value = value + parts[k].astype(F32)
    total[...] = value


def pick_kernel(place, both, text, image):
    core = place[1]
    text[...] = both[0, pl.ds(core, 1)][0]
    image[...] = both[1, pl.ds(core, 1)][0]


def shards(tokens, w1, b1, w2, b2, pictures, matching, sharpness, offset):
    x, core, t = (lax.axis_index(a).astype(jnp.int32) for a in ("x", "core", "t"))
    place = jnp.stack([x, core, t])
    rows, width = pictures.shape
    tensor, ring = lax.axis_size("t"), lax.axis_size("x")
    own = rows // tensor
    groups = lax.axis_size(("yl", "z"))

    bf16, f32 = (functools.partial(jax.ShapeDtypeStruct, dtype=d) for d in (BF16, F32))
    to_all = jnp.broadcast_to(tokens[None], (tensor,) + tokens.shape)
    gathered = lax.all_to_all(to_all, "t", 0, 0)
    spots = jnp.pad(matching.astype(F32), (0, LANES - rows))
    small = jnp.concatenate([spots, b1, b2])[None]
    packed = call(pack_kernel, bf16((rows, width + LANES)), (pictures, small))
    moved = [from_behind(packed, k) for k in range(1, ring)]
    numbers = jnp.concatenate([sharpness, offset])
    partial = call(
        ffn_kernel,
        bf16((tensor, own, width)),
        (gathered, small, w1, w2),
        specs=[VMEM, VMEM, HBM, HBM],
        scratch=[pltpu.VMEM(a.shape, a.dtype) for a in (w1, w2)]
        + [pltpu.SemaphoreType.DMA((2,))],
        room=FULL,
    )
    partial, packed, *moved = lax.optimization_barrier((partial, packed, *moved))
    parts = lax.all_to_all(partial, "t", 0, 0)
    image_own = jnp.concatenate([packed] + moved, axis=0)
    image_other = swap_cores(image_own)
    parts, image_other = lax.optimization_barrier((parts, image_other))
    copies = call(text_kernel, bf16((groups, own, width)), (parts,))
    text_own = lax.all_to_all(copies, ("yl", "z"), 0, 0)
    text_other = swap_cores(text_own)
    shares = call(
        pair_kernel,
        jax.ShapeDtypeStruct((groups, 2, own, width), BF16),
        (place, numbers, text_own, text_other, image_own, image_other),
        scalars=2,
        flops=1_200_000_000,
    )
    shares = lax.all_to_all(shares, ALL, 0, 0, axis_index_groups=grad_groups())
    total = call(sum_kernel, f32((2, own, width)), (shares,))
    both = lax.all_gather(total, "core")
    half = f32((own, width))
    return tuple(call(pick_kernel, (half, half), (place, both), scalars=1))


def solution(mesh):
    fine = Mesh(mesh.devices.reshape([SIZES[a] for a in ALL]), ALL)
    return jax.shard_map(
        shards,
        mesh=fine,
        in_specs=(
            P(ROWS, "t"),
            P(None, "t"),
            P("t"),
            P("t", None),
            P(),
            P(ROWS, None),
            P(ROWS),
            P(),
            P(),
        ),
        out_specs=(P(ALL, None), P(ALL, None)),
        check_vma=False,
    )
```

```python
import functools

import jax
import jax.numpy as jnp
from jax import lax
from jax.experimental import pallas as pl
from jax.experimental.pallas import tpu as pltpu
from jax.sharding import Mesh, PartitionSpec as P

EPSILON = 1e-06
ROWS = ("yl", "z", "x", "core")
ALL = ROWS + ("t",)
SIZES = dict(yl=2, z=8, x=4, core=2, t=4)
BF16 = jnp.bfloat16
F32 = jnp.float32
LANES = 128
VMEM = pl.BlockSpec(memory_space=pltpu.VMEM)
HBM = pl.BlockSpec(memory_space=pl.ANY)
FULL = 55_000_000
SMEM = pl.BlockSpec(memory_space=pltpu.SMEM)


def nt(a, b):
    return lax.dot_general(a, b, (((1,), (1,)), ((), ())), preferred_element_type=F32)


def nn(a, b):
    return jnp.dot(a, b, preferred_element_type=F32)


def call(kernel, outs, operands, scalars=0, flops=0, specs=None, out_specs=None, scratch=(), room=2**25):
    return pl.pallas_call(
        kernel,
        out_shape=outs,
        in_specs=specs or [SMEM] * scalars + [VMEM] * (len(operands) - scalars),
        out_specs=out_specs or jax.tree.map(lambda _: VMEM, outs),
        scratch_shapes=scratch,
        compiler_params=pltpu.CompilerParams(vmem_limit_bytes=room),
        cost_estimate=pl.CostEstimate(flops=flops, bytes_accessed=100_000, transcendentals=0),
    )(*operands)


def swap_cores(block):
    return lax.ppermute(block, "core", [(0, 1), (1, 0)])


def swap_along_x(block, bit):
    return lax.ppermute(block, "x", [(i, i ^ bit) for i in range(lax.axis_size("x"))])


def grad_groups():
    yl, z, x, core, t = (SIZES[a] for a in ALL)

    def flat(i, j, k, c, m):
        return (((i * z + j) * x + k) * core + c) * t + m

    text = [[flat(i, j, k, 0, m) for i in range(yl) for j in range(z)] for k in range(x) for m in range(t)]
    image = [[flat(i, j, k, 1, m) for k in range(x) for m in range(t)] for i in range(yl) for j in range(z)]
    return text + image


def unit(values):
    squared = jnp.sum(values * values, axis=-1, keepdims=True)
    return (values * lax.rsqrt(squared + EPSILON)).astype(BF16)


def pack_kernel(pictures, small, packed):
    count, width = pictures.shape
    packed[:, :width] = unit(pictures[...].astype(F32))
    down = lax.broadcasted_iota(jnp.int32, (count, LANES), 0)
    lane = lax.broadcasted_iota(jnp.int32, (count, LANES), 1)
    where = jnp.sum(jnp.where(down == lane, small[:, :LANES], 0.0), axis=1, keepdims=True).astype(jnp.int32)
    digits = jnp.where(lane == 0, where // LANES, jnp.where(lane == 1, where % LANES, 0))
    packed[:, width:] = digits.astype(F32).astype(BF16)


def ffn_kernel(gathered, small, w1, w2, partial, w1_near, w2_near, sems):
    first = pltpu.make_async_copy(w1, w1_near, sems.at[0])
    second = pltpu.make_async_copy(w2, w2_near, sems.at[1])
    first.start()
    second.start()
    hid = w1.shape[1]
    b1, b2 = small[:, LANES : LANES + hid], small[:, LANES + hid :]
    count = gathered.shape[0]
    tokens = jnp.concatenate([gathered[k].astype(F32) for k in range(count)], axis=1)
    centred = tokens - jnp.mean(tokens, axis=-1, keepdims=True)
    variance = jnp.mean(centred * centred, axis=-1, keepdims=True)
    normed = (centred * lax.rsqrt(variance + EPSILON)).astype(BF16)
    first.wait()
    hidden = jax.nn.gelu(nn(normed, w1_near[...]) + b1, approximate=True).astype(BF16)
    second.wait()
    branch = nn(hidden, w2_near[...])
    total = branch + (tokens + b2) * (1.0 / count)
    partial[...] = total.reshape(partial.shape).astype(partial.dtype)


def text_kernel(parts, copies):
    total = parts[0].astype(F32)
    for k in range(1, parts.shape[0]):
        total = total + parts[k].astype(F32)
    row = unit(total)
    for k in range(copies.shape[0]):
        copies[k] = row


def pair_kernel(place, numbers, text_own, text_other, image_own, image_other, out):
    groups, _, own, width = out.shape
    x, core, t = place[0], place[1], place[2]
    scale, shift = numbers[0], numbers[1]
    ring, tensor = SIZES["x"], SIZES["t"]
    block = tensor * own
    lane = lax.broadcasted_iota(jnp.int32, (8, LANES), 1)
    digit = jnp.where(lane == 0, float(LANES), jnp.where(lane == 1, 1.0, 0.0)).astype(BF16)

    def ids(shape, dim, which):
        row = lax.broadcasted_iota(jnp.int32, shape, dim)
        first = (x * 2 + which) * block + t * own
        return ((row // own) * (ring * 2 * block) + first + row % own).astype(F32)

    def weights(a, b, match):
        scores = scale * nt(a, b) + shift
        score = jnp.where(match, -scores, scores)
        size = jnp.where(match, -scale, scale)
        return (size / (1.0 + jnp.exp(-score))).astype(BF16)

    texts = ((text_own, core), (text_other, 1 - core))
    images = ((image_own, core), (image_other, 1 - core))
    many = groups * own

    @pl.when(core == 0)
    def _():
        for which, (text, from_core) in enumerate(texts):
            a = text[...].reshape(many, width)
            total = None
            for image, _ in images:
                b = image[:, :width]
                position = nt(digit, image[:, width:])[:1]
                match = ids((many, 1), 0, from_core) == position
                part = nn(weights(a, b, match), b)
                total = part if total is None else total + part
            out[:, which] = total.astype(BF16).reshape(groups, own, width)

    @pl.when(core == 1)
    def _():
        for which, (image, from_core) in enumerate(images):
            a = image[:, :width]
            position = nt(image[:, width:], digit)[:, :1]
            total = None
            for text, text_core in texts:
                b = text[...].reshape(many, width)
                match = position == ids((1, many), 1, text_core)
                part = nn(weights(a, b, match), b)
                total = part if total is None else total + part
            total = total.astype(BF16)
            for k, bits in enumerate((0, 2, 1, 3)):
                at = jnp.bitwise_xor(x, bits)
                rows = total[k * block : (k + 1) * block].reshape(tensor, own, width)
                out[pl.ds(at * tensor, tensor), 1 - which] = rows


def sum_kernel(parts, total):
    value = parts[0].astype(F32)
    for k in range(1, parts.shape[0]):
        value = value + parts[k].astype(F32)
    total[...] = value


def shards(tokens, w1, b1, w2, b2, pictures, matching, sharpness, offset):
    x, core, t = (lax.axis_index(a).astype(jnp.int32) for a in ("x", "core", "t"))
    place = jnp.stack([x, core, t])
    rows, width = pictures.shape
    tensor = lax.axis_size("t")
    own = rows // tensor
    groups = lax.axis_size(("yl", "z"))

    bf16, f32 = (functools.partial(jax.ShapeDtypeStruct, dtype=d) for d in (BF16, F32))
    to_all = jnp.broadcast_to(tokens[None], (tensor,) + tokens.shape)
    gathered = lax.all_to_all(to_all, "t", 0, 0)
    spots = jnp.pad(matching.astype(F32), (0, LANES - rows))
    small = jnp.concatenate([spots, b1, b2])[None]
    packed = call(pack_kernel, bf16((rows, width + LANES)), (pictures, small))
    moved = swap_along_x(packed, 2)
    numbers = jnp.concatenate([sharpness, offset])
    partial = call(
        ffn_kernel,
        bf16((tensor, own, width)),
        (gathered, small, w1, w2),
        specs=[VMEM, VMEM, HBM, HBM],
        scratch=[pltpu.VMEM(a.shape, a.dtype) for a in (w1, w2)]
        + [pltpu.SemaphoreType.DMA((2,))],
        room=FULL,
    )
    partial, packed, moved = lax.optimization_barrier((partial, packed, moved))
    couple = jnp.concatenate([packed, moved], axis=0)
    partial, couple = lax.optimization_barrier((partial, couple))
    moved = swap_along_x(couple, 1)
    parts = lax.all_to_all(partial, "t", 0, 0)
    parts, couple, moved = lax.optimization_barrier((parts, couple, moved))
    image_own = jnp.concatenate([couple, moved], axis=0)
    copies = call(text_kernel, bf16((groups, own, width)), (parts,))
    copies, image_own = lax.optimization_barrier((copies, image_own))
    image_other = swap_cores(image_own)
    text_own = lax.all_to_all(copies, ("yl", "z"), 0, 0)
    text_own, image_other, place, numbers, core = lax.optimization_barrier(
        (text_own, image_other, place, numbers, core)
    )
    text_other = swap_cores(text_own)
    shares = call(
        pair_kernel,
        jax.ShapeDtypeStruct((groups, 2, own, width), BF16),
        (place, numbers, text_own, text_other, image_own, image_other),
        scalars=2,
        flops=1_200_000_000,
    )
    shares = lax.all_to_all(shares, ALL, 0, 0, axis_index_groups=grad_groups())
    total = call(sum_kernel, f32((2, own, width)), (shares,))
    both = lax.all_gather(total, "core")
    own_row = functools.partial(
        lax.dynamic_index_in_dim, index=core, keepdims=False, allow_negative_indices=False
    )
    return own_row(both[0]), own_row(both[1])


def solution(mesh):
    fine = Mesh(mesh.devices.reshape([SIZES[a] for a in ALL]), ALL)
    return jax.shard_map(
        shards,
        mesh=fine,
        in_specs=(
            P(ROWS, "t"),
            P(None, "t"),
            P("t"),
            P("t", None),
            P(),
            P(ROWS, None),
            P(ROWS),
            P(),
            P(),
        ),
        out_specs=(P(ALL, None), P(ALL, None)),
        check_vma=False,
    )
```

```python
import functools

import jax
import jax.numpy as jnp
from jax import lax
from jax.experimental import pallas as pl
from jax.experimental.pallas import tpu as pltpu
from jax.sharding import Mesh, PartitionSpec as P

EPSILON = 1e-06
ROWS = ("yl", "z", "x", "core")
ALL = ROWS + ("t",)
SIZES = dict(yl=2, z=8, x=4, core=2, t=4)
BF16 = jnp.bfloat16
F32 = jnp.float32
LANES = 128
VMEM = pl.BlockSpec(memory_space=pltpu.VMEM)
HBM = pl.BlockSpec(memory_space=pl.ANY)
FULL = 55_000_000
SMEM = pl.BlockSpec(memory_space=pltpu.SMEM)


def nt(a, b):
    return lax.dot_general(a, b, (((1,), (1,)), ((), ())), preferred_element_type=F32)


def nn(a, b):
    return jnp.dot(a, b, preferred_element_type=F32)


def call(kernel, outs, operands, scalars=0, flops=0, specs=None, out_specs=None, scratch=(), room=2**25):
    return pl.pallas_call(
        kernel,
        out_shape=outs,
        in_specs=specs or [SMEM] * scalars + [VMEM] * (len(operands) - scalars),
        out_specs=out_specs or jax.tree.map(lambda _: VMEM, outs),
        scratch_shapes=scratch,
        compiler_params=pltpu.CompilerParams(vmem_limit_bytes=room),
        cost_estimate=pl.CostEstimate(flops=flops, bytes_accessed=100_000, transcendentals=0),
    )(*operands)


def swap_cores(block):
    return lax.ppermute(block, "core", [(0, 1), (1, 0)])


def swap_along_x(block, bit):
    return lax.ppermute(block, "x", [(i, i ^ bit) for i in range(lax.axis_size("x"))])


def grad_groups():
    yl, z, x, core, t = (SIZES[a] for a in ALL)

    def flat(i, j, k, c, m):
        return (((i * z + j) * x + k) * core + c) * t + m

    text = [[flat(i, j, k, 0, m) for i in range(yl) for j in range(z)] for k in range(x) for m in range(t)]
    image = [[flat(i, j, k, 1, m) for k in range(x) for m in range(t)] for i in range(yl) for j in range(z)]
    return text + image


def unit(values):
    squared = jnp.sum(values * values, axis=-1, keepdims=True)
    return (values * lax.rsqrt(squared + EPSILON)).astype(BF16)


def pack_kernel(pictures, small, packed):
    count, width = pictures.shape
    packed[:, :width] = unit(pictures[...].astype(F32))
    down = lax.broadcasted_iota(jnp.int32, (count, LANES), 0)
    lane = lax.broadcasted_iota(jnp.int32, (count, LANES), 1)
    where = jnp.sum(jnp.where(down == lane, small[:, :LANES], 0.0), axis=1, keepdims=True).astype(jnp.int32)
    digits = jnp.where(lane == 0, where // LANES, jnp.where(lane == 1, where % LANES, 0))
    packed[:, width:] = digits.astype(F32).astype(BF16)


def ffn_kernel(gathered, small, w1, w2, partial, w1_near, w2_near, sems):
    first = pltpu.make_async_copy(w1, w1_near, sems.at[0])
    second = pltpu.make_async_copy(w2, w2_near, sems.at[1])
    first.start()
    second.start()
    hid = w1.shape[1]
    b1, b2 = small[:, LANES : LANES + hid], small[:, LANES + hid :]
    count = gathered.shape[0]
    tokens = jnp.concatenate([gathered[k].astype(F32) for k in range(count)], axis=1)
    centred = tokens - jnp.mean(tokens, axis=-1, keepdims=True)
    variance = jnp.mean(centred * centred, axis=-1, keepdims=True)
    normed = (centred * lax.rsqrt(variance + EPSILON)).astype(BF16)
    first.wait()
    hidden = jax.nn.gelu(nn(normed, w1_near[...]) + b1, approximate=True).astype(BF16)
    second.wait()
    branch = nn(hidden, w2_near[...])
    total = branch + (tokens + b2) * (1.0 / count)
    partial[...] = total.reshape(partial.shape).astype(partial.dtype)


def text_kernel(parts, copies):
    total = parts[0].astype(F32)
    for k in range(1, parts.shape[0]):
        total = total + parts[k].astype(F32)
    row = unit(total)
    for k in range(copies.shape[0]):
        copies[k] = row


def grad_shares(place, numbers, text, from_other, images, size):
    groups, own, width = text.shape
    x, core, t = place[0], place[1], place[2]
    scale, shift = numbers[0], numbers[1]
    block = SIZES["t"] * own
    many = groups * own
    lane = lax.broadcasted_iota(jnp.int32, (8, LANES), 1)
    digit = jnp.where(lane == 0, float(LANES), jnp.where(lane == 1, 1.0, 0.0)).astype(BF16)
    text_core = (1 - core) if from_other else core
    first = (x * 2 + text_core) * block + t * own

    def ids(shape, dim):
        row = lax.broadcasted_iota(jnp.int32, shape, dim)
        return ((row // own) * (SIZES["x"] * 2 * block) + first + row % own).astype(F32)

    def weights(a, b, match):
        scores = scale * nt(a, b) + shift
        score = jnp.where(match, -scores, scores)
        return (jnp.where(match, -scale, scale) / (1.0 + jnp.exp(-score))).astype(BF16)

    rows = text[...].reshape(many, width)
    if size == 1:
        total = None
        for image in images:
            b = image[:, :width]
            match = ids((many, 1), 0) == nt(digit, image[:, width:])[:1]
            part = nn(weights(rows, b, match), b)
            total = part if total is None else total + part
        return [total]
    shares = []
    for image in images:
        match = nt(image[:, width:], digit)[:, :1] == ids((1, many), 1)
        shares.append(nn(weights(image[:, :width], rows, match), rows))
    return shares


def first_kernel(place, numbers, text, image_own, image_other, held):
    for core in range(2):

        @pl.when(place[1] == core)
        def _():
            shares = grad_shares(place, numbers, text, False, (image_own, image_other), core + 1)
            for k, share in enumerate(shares):
                held[k] = share


def second_kernel(place, numbers, text, image_own, image_other, held, out):
    groups, _, own, width = out.shape
    tensor = SIZES["t"]
    block = tensor * own

    @pl.when(place[1] == 0)
    def _():
        shares = grad_shares(place, numbers, text, True, (image_own, image_other), 1)
        out[:, 0] = held[0].astype(BF16).reshape(groups, own, width)
        out[:, 1] = shares[0].astype(BF16).reshape(groups, own, width)

    @pl.when(place[1] == 1)
    def _():
        shares = grad_shares(place, numbers, text, True, (image_own, image_other), 2)
        for which, share in enumerate(shares):
            total = (held[which] + share).astype(BF16)
            for k, bits in enumerate((0, 2, 1, 3)):
                at = jnp.bitwise_xor(place[0], bits)
                rows = total[k * block : (k + 1) * block].reshape(tensor, own, width)
                out[pl.ds(at * tensor, tensor), 1 - which] = rows


def sum_kernel(parts, total):
    value = parts[0].astype(F32)
    for k in range(1, parts.shape[0]):
        value = value + parts[k].astype(F32)
    total[...] = value


def shards(tokens, w1, b1, w2, b2, pictures, matching, sharpness, offset):
    x, core, t = (lax.axis_index(a).astype(jnp.int32) for a in ("x", "core", "t"))
    place = jnp.stack([x, core, t])
    rows, width = pictures.shape
    tensor = lax.axis_size("t")
    own = rows // tensor
    groups = lax.axis_size(("yl", "z"))

    bf16, f32 = (functools.partial(jax.ShapeDtypeStruct, dtype=d) for d in (BF16, F32))
    to_all = jnp.broadcast_to(tokens[None], (tensor,) + tokens.shape)
    gathered = lax.all_to_all(to_all, "t", 0, 0)
    spots = jnp.pad(matching.astype(F32), (0, LANES - rows))
    small = jnp.concatenate([spots, b1, b2])[None]
    packed = call(pack_kernel, bf16((rows, width + LANES)), (pictures, small))
    moved = swap_along_x(packed, 2)
    numbers = jnp.concatenate([sharpness, offset])
    partial = call(
        ffn_kernel,
        bf16((tensor, own, width)),
        (gathered, small, w1, w2),
        specs=[VMEM, VMEM, HBM, HBM],
        scratch=[pltpu.VMEM(a.shape, a.dtype) for a in (w1, w2)]
        + [pltpu.SemaphoreType.DMA((2,))],
        room=FULL,
    )
    parts = lax.all_to_all(partial, "t", 0, 0)
    couple = jnp.concatenate([packed, moved], axis=0)
    copies = call(text_kernel, bf16((groups, own, width)), (parts,))
    moved = swap_along_x(couple, 1)
    image_own = jnp.concatenate([couple, moved], axis=0)
    image_other = swap_cores(image_own)
    text_own = lax.all_to_all(copies, ("yl", "z"), 0, 0)
    text_own, image_own, image_other, place, numbers, core = lax.optimization_barrier(
        (text_own, image_own, image_other, place, numbers, core)
    )
    text_other = swap_cores(text_own)
    held = call(
        first_kernel,
        f32((2, groups * own, width)),
        (place, numbers, text_own, image_own, image_other),
        scalars=2,
        flops=600_000_000,
    )
    shares = call(
        second_kernel,
        bf16((groups, 2, own, width)),
        (place, numbers, text_other, image_own, image_other, held),
        scalars=2,
        flops=600_000_000,
    )
    shares = lax.all_to_all(shares, ALL, 0, 0, axis_index_groups=grad_groups())
    total = call(sum_kernel, f32((2, own, width)), (shares,))
    both = lax.all_gather(total, "core")
    own_row = functools.partial(
        lax.dynamic_index_in_dim, index=core, keepdims=False, allow_negative_indices=False
    )
    return own_row(both[0]), own_row(both[1])


def solution(mesh):
    fine = Mesh(mesh.devices.reshape([SIZES[a] for a in ALL]), ALL)
    return jax.shard_map(
        shards,
        mesh=fine,
        in_specs=(
            P(ROWS, "t"),
            P(None, "t"),
            P("t"),
            P("t", None),
            P(),
            P(ROWS, None),
            P(ROWS),
            P(),
            P(),
        ),
        out_specs=(P(ALL, None), P(ALL, None)),
        check_vma=False,
    )
```

```python
import functools
import itertools

import jax
import jax.numpy as jnp
from jax import lax
from jax.experimental import pallas as pl
from jax.experimental.pallas import tpu as pltpu
from jax.sharding import Mesh, PartitionSpec as P

EPSILON = 1e-06
ROWS = ("yl", "z", "xh", "xl", "core")
ALL = ROWS + ("t",)
SIZES = dict(yl=2, z=8, xh=2, xl=2, core=2, t=4)
TEXT_GROUP = ("z", "xl")
IMAGE_GROUP = ("yl", "xh", "t")
BF16 = jnp.bfloat16
F32 = jnp.float32
LANES = 128
VMEM = pl.BlockSpec(memory_space=pltpu.VMEM)
HBM = pl.BlockSpec(memory_space=pl.ANY)
FULL = 55_000_000
SMEM = pl.BlockSpec(memory_space=pltpu.SMEM)


def nt(a, b):
    return lax.dot_general(a, b, (((1,), (1,)), ((), ())), preferred_element_type=F32)


def nn(a, b):
    return jnp.dot(a, b, preferred_element_type=F32)


def call(kernel, outs, operands, scalars=0, flops=0, specs=None, out_specs=None, scratch=(), room=2**25):
    return pl.pallas_call(
        kernel,
        out_shape=outs,
        in_specs=specs or [SMEM] * scalars + [VMEM] * (len(operands) - scalars),
        out_specs=out_specs or jax.tree.map(lambda _: VMEM, outs),
        scratch_shapes=scratch,
        compiler_params=pltpu.CompilerParams(vmem_limit_bytes=room),
        cost_estimate=pl.CostEstimate(flops=flops, bytes_accessed=100_000, transcendentals=0),
    )(*operands)


def swap(block, axis):
    return lax.ppermute(block, axis, [(0, 1), (1, 0)])


def grad_groups():
    def groups(core, inside):
        outside = [a for a in ALL if a not in inside and a != "core"]
        out = []
        for fixed in itertools.product(*(range(SIZES[a]) for a in outside)):
            group = []
            for moving in itertools.product(*(range(SIZES[a]) for a in inside)):
                at = dict(zip(outside, fixed), **dict(zip(inside, moving)), core=core)
                number = 0
                for a in ALL:
                    number = number * SIZES[a] + at[a]
                group.append(number)
            out.append(group)
        return out

    return groups(0, TEXT_GROUP) + groups(1, IMAGE_GROUP)


def unit(values):
    squared = jnp.sum(values * values, axis=-1, keepdims=True)
    return (values * lax.rsqrt(squared + EPSILON)).astype(BF16)


def pack_kernel(pictures, small, packed):
    count, width = pictures.shape
    packed[:, :width] = unit(pictures[...].astype(F32))
    down = lax.broadcasted_iota(jnp.int32, (count, LANES), 0)
    lane = lax.broadcasted_iota(jnp.int32, (count, LANES), 1)
    where = jnp.sum(jnp.where(down == lane, small[:, :LANES], 0.0), axis=1, keepdims=True).astype(jnp.int32)
    digits = jnp.where(lane == 0, where // LANES, jnp.where(lane == 1, where % LANES, 0))
    packed[:, width:] = digits.astype(F32).astype(BF16)


def ffn_kernel(gathered, small, w1, w2, partial, w1_near, w2_near, sems):
    first = pltpu.make_async_copy(w1, w1_near, sems.at[0])
    second = pltpu.make_async_copy(w2, w2_near, sems.at[1])
    first.start()
    second.start()
    hid = w1.shape[1]
    b1, b2 = small[:, LANES : LANES + hid], small[:, LANES + hid :]
    count = gathered.shape[0]
    tokens = jnp.concatenate([gathered[k].astype(F32) for k in range(count)], axis=1)
    centred = tokens - jnp.mean(tokens, axis=-1, keepdims=True)
    variance = jnp.mean(centred * centred, axis=-1, keepdims=True)
    normed = (centred * lax.rsqrt(variance + EPSILON)).astype(BF16)
    first.wait()
    hidden = jax.nn.gelu(nn(normed, w1_near[...]) + b1, approximate=True).astype(BF16)
    second.wait()
    branch = nn(hidden, w2_near[...])
    total = branch + (tokens + b2) * (1.0 / count)
    partial[...] = total.reshape(partial.shape).astype(partial.dtype)


def text_kernel(parts, copies):
    total = parts[0].astype(F32)
    for k in range(1, parts.shape[0]):
        total = total + parts[k].astype(F32)
    row = unit(total)
    for k in range(copies.shape[0]):
        copies[k] = row


def grad_shares(place, numbers, text, from_other, images, size):
    groups, own, width = text.shape
    yl, core, t, xbit = place[0], place[1], place[2], place[3]
    scale, shift = numbers[0], numbers[1]
    block = SIZES["t"] * own
    many = groups * own
    lane = lax.broadcasted_iota(jnp.int32, (8, LANES), 1)
    digit = jnp.where(lane == 0, float(LANES), jnp.where(lane == 1, 1.0, 0.0)).astype(BF16)
    text_core = (1 - core) if from_other else core
    chip_row = 8 * block
    first = yl * (SIZES["z"] * chip_row) + (xbit * 4 + text_core) * block + t * own

    def ids(shape, dim):
        row = lax.broadcasted_iota(jnp.int32, shape, dim)
        member = row // own
        return ((member // 2) * chip_row + (member % 2) * (2 * block) + first + row % own).astype(F32)

    def weights(a, b, match):
        scores = scale * nt(a, b) + shift
        score = jnp.where(match, -scores, scores)
        return (jnp.where(match, -scale, scale) / (1.0 + jnp.exp(-score))).astype(BF16)

    rows = text[...].reshape(many, width)
    if size == 1:
        total = None
        for image in images:
            b = image[:, :width]
            match = ids((many, 1), 0) == nt(digit, image[:, width:])[:1]
            part = nn(weights(rows, b, match), b)
            total = part if total is None else total + part
        return [total]
    shares = []
    for image in images:
        match = nt(image[:, width:], digit)[:, :1] == ids((1, many), 1)
        shares.append(nn(weights(image[:, :width], rows, match), rows))
    return shares


def first_kernel(place, numbers, text, image_own, image_other, held):
    for core in range(2):

        @pl.when(place[1] == core)
        def _():
            shares = grad_shares(place, numbers, text, False, (image_own, image_other), core + 1)
            for k, share in enumerate(shares):
                held[k] = share


def second_kernel(place, numbers, text, image_own, image_other, held, out):
    groups, _, own, width = out.shape
    tensor = SIZES["t"]
    block = tensor * own

    @pl.when(place[1] == 0)
    def _():
        shares = grad_shares(place, numbers, text, True, (image_own, image_other), 1)
        out[:, 0] = held[0].astype(BF16).reshape(groups, own, width)
        out[:, 1] = shares[0].astype(BF16).reshape(groups, own, width)

    @pl.when(place[1] == 1)
    def _():
        shares = grad_shares(place, numbers, text, True, (image_own, image_other), 2)
        for which, share in enumerate(shares):
            total = (held[which] + share).astype(BF16)
            for k in range(4):
                at = jnp.bitwise_xor(place[0], k % 2) * 2 + jnp.bitwise_xor(place[3], k // 2)
                rows = total[k * block : (k + 1) * block].reshape(tensor, own, width)
                out[pl.ds(at * tensor, tensor), 1 - which] = rows


def sum_kernel(parts, total):
    value = parts[0].astype(F32)
    for k in range(1, parts.shape[0]):
        value = value + parts[k].astype(F32)
    total[...] = value


def shards(tokens, w1, b1, w2, b2, pictures, matching, sharpness, offset):
    axes = ("yl", "core", "t", IMAGE_GROUP[1])
    yl, core, t, xbit = (lax.axis_index(a).astype(jnp.int32) for a in axes)
    place = jnp.stack([yl, core, t, xbit])
    rows, width = pictures.shape
    tensor = lax.axis_size("t")
    own = rows // tensor
    groups = lax.axis_size(TEXT_GROUP)

    bf16, f32 = (functools.partial(jax.ShapeDtypeStruct, dtype=d) for d in (BF16, F32))
    to_all = jnp.broadcast_to(tokens[None], (tensor,) + tokens.shape)
    gathered = lax.all_to_all(to_all, "t", 0, 0)
    spots = jnp.pad(matching.astype(F32), (0, LANES - rows))
    small = jnp.concatenate([spots, b1, b2])[None]
    packed = call(pack_kernel, bf16((rows, width + LANES)), (pictures, small))
    moved = swap(packed, "yl")
    numbers = jnp.concatenate([sharpness, offset])
    partial = call(
        ffn_kernel,
        bf16((tensor, own, width)),
        (gathered, small, w1, w2),
        specs=[VMEM, VMEM, HBM, HBM],
        scratch=[pltpu.VMEM(a.shape, a.dtype) for a in (w1, w2)]
        + [pltpu.SemaphoreType.DMA((2,))],
        room=FULL,
    )
    parts = lax.all_to_all(partial, "t", 0, 0)
    couple = jnp.concatenate([packed, moved], axis=0)
    copies = call(text_kernel, bf16((groups, own, width)), (parts,))
    moved = swap(couple, IMAGE_GROUP[1])
    image_own = jnp.concatenate([couple, moved], axis=0)
    image_other = swap(image_own, "core")
    text_own = lax.all_to_all(copies, TEXT_GROUP, 0, 0)
    text_own, image_own, image_other, place, numbers, core = lax.optimization_barrier(
        (text_own, image_own, image_other, place, numbers, core)
    )
    text_other = swap(text_own, "core")
    held = call(
        first_kernel,
        f32((2, groups * own, width)),
        (place, numbers, text_own, image_own, image_other),
        scalars=2,
        flops=600_000_000,
    )
    shares = call(
        second_kernel,
        bf16((groups, 2, own, width)),
        (place, numbers, text_other, image_own, image_other, held),
        scalars=2,
        flops=600_000_000,
    )
    shares = lax.all_to_all(shares, ALL, 0, 0, axis_index_groups=grad_groups())
    total = call(sum_kernel, f32((2, own, width)), (shares,))
    both = lax.all_gather(total, "core")
    own_row = functools.partial(
        lax.dynamic_index_in_dim, index=core, keepdims=False, allow_negative_indices=False
    )
    return own_row(both[0]), own_row(both[1])


def solution(mesh):
    fine = Mesh(mesh.devices.reshape([SIZES[a] for a in ALL]), ALL)
    return jax.shard_map(
        shards,
        mesh=fine,
        in_specs=(
            P(ROWS, "t"),
            P(None, "t"),
            P("t"),
            P("t", None),
            P(),
            P(ROWS, None),
            P(ROWS),
            P(),
            P(),
        ),
        out_specs=(P(ALL, None), P(ALL, None)),
        check_vma=False,
    )
```

```python
import functools
import itertools

import jax
import jax.numpy as jnp
from jax import lax
from jax.experimental import pallas as pl
from jax.experimental.pallas import tpu as pltpu
from jax.sharding import Mesh, PartitionSpec as P

EPSILON = 1e-06
ROWS = ("yl", "z", "xh", "xl", "core")
ALL = ROWS + ("t",)
SIZES = dict(yl=2, z=8, xh=2, xl=2, core=2, t=4)
TEXT_GROUP = ("xl", "z")
IMAGE_GROUP = ("xh", "yl", "t")
BF16 = jnp.bfloat16
F32 = jnp.float32
LANES = 128
VMEM = pl.BlockSpec(memory_space=pltpu.VMEM)
HBM = pl.BlockSpec(memory_space=pl.ANY)
FULL = 55_000_000
SMEM = pl.BlockSpec(memory_space=pltpu.SMEM)


def nt(a, b):
    return lax.dot_general(a, b, (((1,), (1,)), ((), ())), preferred_element_type=F32)


def nn(a, b):
    return jnp.dot(a, b, preferred_element_type=F32)


def call(kernel, outs, operands, scalars=0, flops=0, specs=None, out_specs=None, scratch=(), room=2**25):
    return pl.pallas_call(
        kernel,
        out_shape=outs,
        in_specs=specs or [SMEM] * scalars + [VMEM] * (len(operands) - scalars),
        out_specs=out_specs or jax.tree.map(lambda _: VMEM, outs),
        scratch_shapes=scratch,
        compiler_params=pltpu.CompilerParams(vmem_limit_bytes=room),
        cost_estimate=pl.CostEstimate(flops=flops, bytes_accessed=100_000, transcendentals=0),
    )(*operands)


def swap(block, axis):
    return lax.ppermute(block, axis, [(0, 1), (1, 0)])


def grad_groups():
    def groups(core, inside):
        outside = [a for a in ALL if a not in inside and a != "core"]
        out = []
        for fixed in itertools.product(*(range(SIZES[a]) for a in outside)):
            group = []
            for moving in itertools.product(*(range(SIZES[a]) for a in inside)):
                at = dict(zip(outside, fixed), **dict(zip(inside, moving)), core=core)
                number = 0
                for a in ALL:
                    number = number * SIZES[a] + at[a]
                group.append(number)
            out.append(group)
        return out

    return groups(0, TEXT_GROUP) + groups(1, IMAGE_GROUP)


def unit(values):
    squared = jnp.sum(values * values, axis=-1, keepdims=True)
    return (values * lax.rsqrt(squared + EPSILON)).astype(BF16)


def pack_kernel(pictures, small, packed):
    count, width = pictures.shape
    packed[:, :width] = unit(pictures[...].astype(F32))
    down = lax.broadcasted_iota(jnp.int32, (count, LANES), 0)
    lane = lax.broadcasted_iota(jnp.int32, (count, LANES), 1)
    where = jnp.sum(jnp.where(down == lane, small[:, :LANES], 0.0), axis=1, keepdims=True).astype(jnp.int32)
    digits = jnp.where(lane == 0, where // LANES, jnp.where(lane == 1, where % LANES, 0))
    packed[:, width:] = digits.astype(F32).astype(BF16)


def ffn_kernel(gathered, small, w1, w2, partial, w1_near, w2_near, sems):
    first = pltpu.make_async_copy(w1, w1_near, sems.at[0])
    second = pltpu.make_async_copy(w2, w2_near, sems.at[1])
    first.start()
    second.start()
    hid = w1.shape[1]
    b1, b2 = small[:, LANES : LANES + hid], small[:, LANES + hid :]
    count = gathered.shape[0]
    tokens = jnp.concatenate([gathered[k].astype(F32) for k in range(count)], axis=1)
    centred = tokens - jnp.mean(tokens, axis=-1, keepdims=True)
    variance = jnp.mean(centred * centred, axis=-1, keepdims=True)
    normed = (centred * lax.rsqrt(variance + EPSILON)).astype(BF16)
    first.wait()
    hidden = jax.nn.gelu(nn(normed, w1_near[...]) + b1, approximate=True).astype(BF16)
    second.wait()
    branch = nn(hidden, w2_near[...])
    total = branch + (tokens + b2) * (1.0 / count)
    partial[...] = total.reshape(partial.shape).astype(partial.dtype)


def text_kernel(parts, copies):
    total = parts[0].astype(F32)
    for k in range(1, parts.shape[0]):
        total = total + parts[k].astype(F32)
    row = unit(total)
    for k in range(copies.shape[0]):
        copies[k] = row


def grad_shares(place, numbers, text, from_other, images, size):
    groups, own, width = text.shape
    yl, core, t, xbit = place[0], place[1], place[2], place[3]
    scale, shift = numbers[0], numbers[1]
    block = SIZES["t"] * own
    many = groups * own
    lane = lax.broadcasted_iota(jnp.int32, (8, LANES), 1)
    digit = jnp.where(lane == 0, float(LANES), jnp.where(lane == 1, 1.0, 0.0)).astype(BF16)
    text_core = (1 - core) if from_other else core
    chip_row = 8 * block
    first = yl * (SIZES["z"] * chip_row) + (xbit * 4 + text_core) * block + t * own

    def ids(shape, dim):
        row = lax.broadcasted_iota(jnp.int32, shape, dim)
        member = row // own
        xl, z = member // SIZES["z"], member % SIZES["z"]
        return (z * chip_row + xl * (2 * block) + first + row % own).astype(F32)

    def weights(a, b, match):
        scores = scale * nt(a, b) + shift
        score = jnp.where(match, -scores, scores)
        return (jnp.where(match, -scale, scale) / (1.0 + jnp.exp(-score))).astype(BF16)

    rows = text[...].reshape(many, width)
    if size == 1:
        total = None
        for image in images:
            b = image[:, :width]
            match = ids((many, 1), 0) == nt(digit, image[:, width:])[:1]
            part = nn(weights(rows, b, match), b)
            total = part if total is None else total + part
        return [total]
    shares = []
    for image in images:
        match = nt(image[:, width:], digit)[:, :1] == ids((1, many), 1)
        shares.append(nn(weights(image[:, :width], rows, match), rows))
    return shares


def first_kernel(place, numbers, text, image_own, image_other, held):
    for core in range(2):

        @pl.when(place[1] == core)
        def _():
            shares = grad_shares(place, numbers, text, False, (image_own, image_other), core + 1)
            for k, share in enumerate(shares):
                held[k] = share


def second_kernel(place, numbers, text, image_own, image_other, held, out):
    groups, _, own, width = out.shape
    tensor = SIZES["t"]
    block = tensor * own

    @pl.when(place[1] == 0)
    def _():
        shares = grad_shares(place, numbers, text, True, (image_own, image_other), 1)
        out[:, 0] = held[0].astype(BF16).reshape(groups, own, width)
        out[:, 1] = shares[0].astype(BF16).reshape(groups, own, width)

    @pl.when(place[1] == 1)
    def _():
        shares = grad_shares(place, numbers, text, True, (image_own, image_other), 2)
        for which, share in enumerate(shares):
            total = (held[which] + share).astype(BF16)
            for k in range(4):
                at = jnp.bitwise_xor(place[3], k // 2) * 2 + jnp.bitwise_xor(place[0], k % 2)
                rows = total[k * block : (k + 1) * block].reshape(tensor, own, width)
                out[pl.ds(at * tensor, tensor), 1 - which] = rows


def sum_kernel(parts, total):
    value = parts[0].astype(F32)
    for k in range(1, parts.shape[0]):
        value = value + parts[k].astype(F32)
    total[...] = value


def shards(tokens, w1, b1, w2, b2, pictures, matching, sharpness, offset):
    axes = ("yl", "core", "t", "xh")
    yl, core, t, xbit = (lax.axis_index(a).astype(jnp.int32) for a in axes)
    place = jnp.stack([yl, core, t, xbit])
    rows, width = pictures.shape
    tensor = lax.axis_size("t")
    own = rows // tensor
    groups = lax.axis_size(TEXT_GROUP)

    bf16, f32 = (functools.partial(jax.ShapeDtypeStruct, dtype=d) for d in (BF16, F32))
    to_all = jnp.broadcast_to(tokens[None], (tensor,) + tokens.shape)
    gathered = lax.all_to_all(to_all, "t", 0, 0)
    spots = jnp.pad(matching.astype(F32), (0, LANES - rows))
    small = jnp.concatenate([spots, b1, b2])[None]
    packed = call(pack_kernel, bf16((rows, width + LANES)), (pictures, small))
    moved = swap(packed, "yl")
    numbers = jnp.concatenate([sharpness, offset])
    partial = call(
        ffn_kernel,
        bf16((tensor, own, width)),
        (gathered, small, w1, w2),
        specs=[VMEM, VMEM, HBM, HBM],
        scratch=[pltpu.VMEM(a.shape, a.dtype) for a in (w1, w2)]
        + [pltpu.SemaphoreType.DMA((2,))],
        room=FULL,
    )
    parts = lax.all_to_all(partial, "t", 0, 0)
    couple = jnp.concatenate([packed, moved], axis=0)
    copies = call(text_kernel, bf16((groups, own, width)), (parts,))
    moved = swap(couple, "xh")
    image_own = jnp.concatenate([couple, moved], axis=0)
    image_other = swap(image_own, "core")
    text_own = lax.all_to_all(copies, TEXT_GROUP, 0, 0)
    text_own, image_own, image_other, place, numbers, core = lax.optimization_barrier(
        (text_own, image_own, image_other, place, numbers, core)
    )
    text_other = swap(text_own, "core")
    held = call(
        first_kernel,
        f32((2, groups * own, width)),
        (place, numbers, text_own, image_own, image_other),
        scalars=2,
        flops=600_000_000,
    )
    shares = call(
        second_kernel,
        bf16((groups, 2, own, width)),
        (place, numbers, text_other, image_own, image_other, held),
        scalars=2,
        flops=600_000_000,
    )
    shares = lax.all_to_all(shares, ALL, 0, 0, axis_index_groups=grad_groups())
    total = call(sum_kernel, f32((2, own, width)), (shares,))
    both = lax.all_gather(total, "core")
    own_row = functools.partial(
        lax.dynamic_index_in_dim, index=core, keepdims=False, allow_negative_indices=False
    )
    return own_row(both[0]), own_row(both[1])


def solution(mesh):
    fine = Mesh(mesh.devices.reshape([SIZES[a] for a in ALL]), ALL)
    return jax.shard_map(
        shards,
        mesh=fine,
        in_specs=(
            P(ROWS, "t"),
            P(None, "t"),
            P("t"),
            P("t", None),
            P(),
            P(ROWS, None),
            P(ROWS),
            P(),
            P(),
        ),
        out_specs=(P(ALL, None), P(ALL, None)),
        check_vma=False,
    )
```

```python
import functools
import itertools

import jax
import jax.numpy as jnp
from jax import lax
from jax.experimental import pallas as pl
from jax.experimental.pallas import tpu as pltpu
from jax.sharding import Mesh, PartitionSpec as P

EPSILON = 1e-06
ROWS = ("yl", "z", "xh", "xl", "core")
ALL = ROWS + ("t",)
SIZES = dict(yl=2, z=8, xh=2, xl=2, core=2, t=4)
TEXT_GROUP = ("xl", "z")
IMAGE_GROUP = ("xh", "yl", "t")
BF16 = jnp.bfloat16
F32 = jnp.float32
LANES = 128
CHUNKS = 4
VMEM = pl.BlockSpec(memory_space=pltpu.VMEM)
HBM = pl.BlockSpec(memory_space=pl.ANY)
FULL = 55_000_000
SMEM = pl.BlockSpec(memory_space=pltpu.SMEM)


def nt(a, b):
    return lax.dot_general(a, b, (((1,), (1,)), ((), ())), preferred_element_type=F32)


def nn(a, b):
    return jnp.dot(a, b, preferred_element_type=F32)


def call(kernel, outs, operands, scalars=0, flops=0, specs=None, out_specs=None, scratch=(), room=2**25):
    return pl.pallas_call(
        kernel,
        out_shape=outs,
        in_specs=specs or [SMEM] * scalars + [VMEM] * (len(operands) - scalars),
        out_specs=out_specs or jax.tree.map(lambda _: VMEM, outs),
        scratch_shapes=scratch,
        compiler_params=pltpu.CompilerParams(vmem_limit_bytes=room),
        cost_estimate=pl.CostEstimate(flops=flops, bytes_accessed=100_000, transcendentals=0),
    )(*operands)


def swap(block, axis):
    return lax.ppermute(block, axis, [(0, 1), (1, 0)])


def grad_groups():
    def groups(core, inside):
        outside = [a for a in ALL if a not in inside and a != "core"]
        out = []
        for fixed in itertools.product(*(range(SIZES[a]) for a in outside)):
            group = []
            for moving in itertools.product(*(range(SIZES[a]) for a in inside)):
                at = dict(zip(outside, fixed), **dict(zip(inside, moving)), core=core)
                number = 0
                for a in ALL:
                    number = number * SIZES[a] + at[a]
                group.append(number)
            out.append(group)
        return out

    return groups(0, TEXT_GROUP) + groups(1, IMAGE_GROUP)


def unit(values):
    squared = jnp.sum(values * values, axis=-1, keepdims=True)
    return (values * lax.rsqrt(squared + EPSILON)).astype(BF16)


def pack_kernel(pictures, small, packed):
    count, width = pictures.shape
    packed[:, :width] = unit(pictures[...].astype(F32))
    down = lax.broadcasted_iota(jnp.int32, (count, LANES), 0)
    lane = lax.broadcasted_iota(jnp.int32, (count, LANES), 1)
    where = jnp.sum(jnp.where(down == lane, small[:, :LANES], 0.0), axis=1, keepdims=True).astype(jnp.int32)
    digits = jnp.where(lane == 0, where // LANES, jnp.where(lane == 1, where % LANES, 0))
    packed[:, width:] = digits.astype(F32).astype(BF16)


def ffn_kernel(gathered, small, w1, w2, partial, w1_near, w2_near, sems):
    def fetch(far, near, base):
        step = far.shape[0] // CHUNKS
        copies = []
        for k in range(CHUNKS):
            part = pl.ds(k * step, step)
            copies.append(pltpu.make_async_copy(far.at[part], near.at[part], sems.at[base + k]))
        for copy in copies:
            copy.start()
        return copies

    first = fetch(w1, w1_near, 0)
    second = fetch(w2, w2_near, CHUNKS)
    hid = w1.shape[1]
    b1, b2 = small[:, LANES : LANES + hid], small[:, LANES + hid :]
    count = gathered.shape[0]
    tokens = jnp.concatenate([gathered[k].astype(F32) for k in range(count)], axis=1)
    centred = tokens - jnp.mean(tokens, axis=-1, keepdims=True)
    variance = jnp.mean(centred * centred, axis=-1, keepdims=True)
    normed = (centred * lax.rsqrt(variance + EPSILON)).astype(BF16)
    for copy in first:
        copy.wait()
    hidden = jax.nn.gelu(nn(normed, w1_near[...]) + b1, approximate=True).astype(BF16)
    for copy in second:
        copy.wait()
    branch = nn(hidden, w2_near[...])
    total = branch + (tokens + b2) * (1.0 / count)
    partial[...] = total.reshape(partial.shape).astype(partial.dtype)


def text_kernel(parts, copies):
    total = parts[0].astype(F32)
    for k in range(1, parts.shape[0]):
        total = total + parts[k].astype(F32)
    row = unit(total)
    for k in range(copies.shape[0]):
        copies[k] = row


def grad_shares(place, numbers, text, from_other, images, size):
    groups, own, width = text.shape
    yl, core, t, xbit = place[0], place[1], place[2], place[3]
    scale, shift = numbers[0], numbers[1]
    block = SIZES["t"] * own
    many = groups * own
    lane = lax.broadcasted_iota(jnp.int32, (8, LANES), 1)
    digit = jnp.where(lane == 0, float(LANES), jnp.where(lane == 1, 1.0, 0.0)).astype(BF16)
    text_core = (1 - core) if from_other else core
    chip_row = 8 * block
    first = yl * (SIZES["z"] * chip_row) + (xbit * 4 + text_core) * block + t * own

    def ids(shape, dim):
        row = lax.broadcasted_iota(jnp.int32, shape, dim)
        member = row // own
        xl, z = member // SIZES["z"], member % SIZES["z"]
        return (z * chip_row + xl * (2 * block) + first + row % own).astype(F32)

    def weights(a, b, match):
        scores = scale * nt(a, b) + shift
        score = jnp.where(match, -scores, scores)
        return (jnp.where(match, -scale, scale) / (1.0 + jnp.exp(-score))).astype(BF16)

    rows = text[...].reshape(many, width)
    if size == 1:
        total = None
        for image in images:
            b = image[:, :width]
            match = ids((many, 1), 0) == nt(digit, image[:, width:])[:1]
            part = nn(weights(rows, b, match), b)
            total = part if total is None else total + part
        return [total]
    shares = []
    for image in images:
        match = nt(image[:, width:], digit)[:, :1] == ids((1, many), 1)
        shares.append(nn(weights(image[:, :width], rows, match), rows))
    return shares


def first_kernel(place, numbers, text, image_own, image_other, held):
    for core in range(2):

        @pl.when(place[1] == core)
        def _():
            shares = grad_shares(place, numbers, text, False, (image_own, image_other), core + 1)
            for k, share in enumerate(shares):
                held[k] = share


def second_kernel(place, numbers, text, image_own, image_other, held, out):
    groups, _, own, width = out.shape
    tensor = SIZES["t"]
    block = tensor * own

    @pl.when(place[1] == 0)
    def _():
        shares = grad_shares(place, numbers, text, True, (image_own, image_other), 1)
        out[:, 0] = held[0].astype(BF16).reshape(groups, own, width)
        out[:, 1] = shares[0].astype(BF16).reshape(groups, own, width)

    @pl.when(place[1] == 1)
    def _():
        shares = grad_shares(place, numbers, text, True, (image_own, image_other), 2)
        for which, share in enumerate(shares):
            total = (held[which] + share).astype(BF16)
            for k in range(4):
                at = jnp.bitwise_xor(place[3], k // 2) * 2 + jnp.bitwise_xor(place[0], k % 2)
                rows = total[k * block : (k + 1) * block].reshape(tensor, own, width)
                out[pl.ds(at * tensor, tensor), 1 - which] = rows


def sum_kernel(parts, total):
    value = parts[0].astype(F32)
    for k in range(1, parts.shape[0]):
        value = value + parts[k].astype(F32)
    total[...] = value


def shards(tokens, w1, b1, w2, b2, pictures, matching, sharpness, offset):
    axes = ("yl", "core", "t", "xh")
    yl, core, t, xbit = (lax.axis_index(a).astype(jnp.int32) for a in axes)
    place = jnp.stack([yl, core, t, xbit])
    rows, width = pictures.shape
    tensor = lax.axis_size("t")
    own = rows // tensor
    groups = lax.axis_size(TEXT_GROUP)

    bf16, f32 = (functools.partial(jax.ShapeDtypeStruct, dtype=d) for d in (BF16, F32))
    to_all = jnp.broadcast_to(tokens[None], (tensor,) + tokens.shape)
    gathered = lax.all_to_all(to_all, "t", 0, 0)
    spots = jnp.pad(matching.astype(F32), (0, LANES - rows))
    small = jnp.concatenate([spots, b1, b2])[None]
    packed = call(pack_kernel, bf16((rows, width + LANES)), (pictures, small))
    moved = swap(packed, "yl")
    numbers = jnp.concatenate([sharpness, offset])
    partial = call(
        ffn_kernel,
        bf16((tensor, own, width)),
        (gathered, small, w1, w2),
        specs=[VMEM, VMEM, HBM, HBM],
        scratch=[pltpu.VMEM(a.shape, a.dtype) for a in (w1, w2)]
        + [pltpu.SemaphoreType.DMA((2 * CHUNKS,))],
        room=FULL,
    )
    parts = lax.all_to_all(partial, "t", 0, 0)
    couple = jnp.concatenate([packed, moved], axis=0)
    copies = call(text_kernel, bf16((groups, own, width)), (parts,))
    moved = swap(couple, "xh")
    image_own = jnp.concatenate([couple, moved], axis=0)
    image_other = swap(image_own, "core")
    text_own = lax.all_to_all(copies, TEXT_GROUP, 0, 0)
    text_own, image_own, image_other, place, numbers, core = lax.optimization_barrier(
        (text_own, image_own, image_other, place, numbers, core)
    )
    text_other = swap(text_own, "core")
    held = call(
        first_kernel,
        f32((2, groups * own, width)),
        (place, numbers, text_own, image_own, image_other),
        scalars=2,
        flops=600_000_000,
    )
    shares = call(
        second_kernel,
        bf16((groups, 2, own, width)),
        (place, numbers, text_other, image_own, image_other, held),
        scalars=2,
        flops=600_000_000,
    )
    shares = lax.all_to_all(shares, ALL, 0, 0, axis_index_groups=grad_groups())
    total = call(sum_kernel, f32((2, own, width)), (shares,))
    both = lax.all_gather(total, "core")
    own_row = functools.partial(
        lax.dynamic_index_in_dim, index=core, keepdims=False, allow_negative_indices=False
    )
    return own_row(both[0]), own_row(both[1])


def solution(mesh):
    fine = Mesh(mesh.devices.reshape([SIZES[a] for a in ALL]), ALL)
    return jax.shard_map(
        shards,
        mesh=fine,
        in_specs=(
            P(ROWS, "t"),
            P(None, "t"),
            P("t"),
            P("t", None),
            P(),
            P(ROWS, None),
            P(ROWS),
            P(),
            P(),
        ),
        out_specs=(P(ALL, None), P(ALL, None)),
        check_vma=False,
    )
```
